512 devices in a mesh: roll: 64 (over z, x_lo, core), head: 8 (over x_hi, y).
Axes of the slice: x: 4 (x_hi: 2, x_lo: 2; x = x_hi * 2 + x_lo), y: 4, z: 16, core: 2. Of those that a mesh axis runs over, the one named last changes fastest.
Arguments:
- query: bfloat16 [64, 128, 8192], P('roll', None, 'head'), may hold values from -48 to 48
- resp_kv: bfloat16 [64, 128, 2048], P('roll', None, 'head'), may hold values from -6 to 6
- grad_out: bfloat16 [64, 128, 8192], P('roll', None, 'head'), may hold values from -6 to 6
- prefix_kv: bfloat16 [4096, 2048], P('roll', 'head'), may hold values from -6 to 6
- lengths: int32 [64], replicated, may hold values from 1 to 128, 5120 in all
- order: int32 [64], P('roll'), may hold values from 0 to 63, each once
Outputs:
- d_query: bfloat16 [64, 128, 8192], P('roll', None, 'head')
- d_resp_kv: bfloat16 [64, 128, 2048], P('roll', 'head')
- d_prefix: float32 [4096, 2048], P('roll', 'head')
The draws below stay inside these ranges and needn't reach their ends.
Inputs may be any that keep to these rules, and one draw needn't show every extreme that they name: order holds each response number once.
All inputs are finite; a program needn't handle non-finite values.
Results may differ from the reference program's by a relative error of at most 0.012.
The reference program's roundings to bfloat16 on the way count: a program that leaves them out, or rounds other values in their place, can miss the bound.
Values may be sent and summed in bfloat16 or wider, within the bound.
No kernel may reach another device: no remote copies, remote signals or barrier semaphores. Data moves between devices by JAX's collectives and lax.ppermute only.
A program may use at most 64 MiB of HBM per device.

```python
import math
import jax
import jax.numpy as jnp
import numpy as np
from jax import lax

HD = 128
GROUP = 8
KVH = 8
QH = 64
RMAX = 128
NRESP = 64
PROMPT = 4096


def shared_keys(key):
    return jnp.clip(jax.random.normal(key, (NRESP, RMAX, KVH, HD), jnp.float32), -6.0, 6.0)


def draw_resp_kv(key, part):
    keys = shared_keys(key)
    key = jax.random.fold_in(key, 11)
    shape = (NRESP, RMAX, KVH, HD)
    values = jnp.clip(jax.random.normal(key, shape, jnp.float32), -6.0, 6.0)
    both = jnp.stack([keys, values], 3)
    return both.reshape(NRESP, RMAX, KVH * 2 * HD).astype(jnp.bfloat16)


def draw_query(key, part):
    key = jax.random.fold_in(key, 7)
    shape = (NRESP, RMAX, KVH, GROUP, HD)
    base = jax.random.normal(key, shape, jnp.float32)
    return jnp.clip(base, -48.0, 48.0).reshape(NRESP, RMAX, KVH * GROUP * HD).astype(jnp.bfloat16)


def block_scale(rng, shape, cuts, smallest, largest):
    gain = 1.0
    for dim, blocks in cuts:
        steps = jax.random.uniform(jax.random.fold_in(jax.random.fold_in(rng, 6), dim), (blocks,), jnp.float32, smallest / len(cuts), largest / len(cuts))
        gain = gain * jnp.repeat(jnp.exp(steps), shape[dim] // blocks).reshape((-1,) + (1,) * (len(shape) - 1 - dim))
    return gain


def split_up(count, total, limit, skew):
    weights = [(1 << 20) // math.isqrt(standing ** skew) + 1 for standing in range(2, count + 1)]
    rest, holding = total - limit - (count - 1), [1] * (count - 1)
    while rest > 0:
        candidates = [i for i in range(count - 1) if holding[i] < limit]
        pool, budget = sum([weights[i] for i in candidates]), rest
        for i in candidates:
            addition = min(limit - holding[i], max(1, budget * weights[i] // pool), rest)
            holding[i] = holding[i] + addition
            rest = rest - addition
    return np.array([limit] + holding)


def uneven(own_key, amount, total, reach, slope):
    if amount == 2:
        one = jax.random.randint(own_key, (), max(1, total - reach), min(reach, total - 1) + 1)
        return jnp.stack([one, total - one])
    sizes = jnp.asarray(split_up(amount, total, reach, slope), jnp.int32)
    couples = (amount - 1) // 2
    giver, taker = sizes[1:1 + 2 * couples:2], sizes[2:2 + 2 * couples:2]
    slack = jnp.minimum(giver - 1, reach - taker)
    passed = jax.random.randint(jax.random.fold_in(own_key, 1), (couples,), 0, 1 << 20) % (slack + 1)
    sizes = sizes.at[1:1 + 2 * couples:2].set(giver - passed).at[2:2 + 2 * couples:2].set(taker + passed)
    return sizes[jax.random.permutation(jax.random.fold_in(own_key, 2), amount)]


def scatter_about(stream_key, extent, width, bound, split=(), held_as=jnp.bfloat16):
    values = width * jax.random.normal(stream_key, extent, jnp.float32)
    if split:
        values = values * block_scale(stream_key, extent, split, -0.22, 0.18)
    return jnp.clip(values, -bound, bound).astype(held_as)


def setup_inputs(seed: int = 0) -> dict:
    splits = jax.random.split(jax.random.key(seed), 7)
    return {
        "query": draw_query(jax.random.fold_in(splits[6], 71), 0),
        "resp_kv": draw_resp_kv(jax.random.fold_in(splits[6], 71), 0),
        "grad_out": scatter_about(splits[2], (NRESP, RMAX, QH * HD), 1.0, 6.0, ((0, 64), (2, 8))),
        "prefix_kv": scatter_about(splits[3], (PROMPT, KVH * 2 * HD), 1.0, 6.0, ((0, 64), (1, 8))),
        "lengths": uneven(splits[4], NRESP, NRESP * RMAX * 5 // 8, RMAX, 2).astype(jnp.int32),
        "order": jax.random.permutation(splits[5], NRESP).astype(jnp.int32),
    }


def rounded(values):
    return lax.optimization_barrier(values.astype(jnp.bfloat16)).astype(jnp.float32)

def response_grads(query_matrix, kv_rows, gradient_list, live, prompt_keys, prompt_values):
    score_scale = 1.0 / math.sqrt(HD)
    response_keys = kv_rows[:, :, 0]
    response_values = kv_rows[:, :, 1]
    prompt_scores = jnp.einsum('lhgd,phd->hglp', query_matrix, prompt_keys) * score_scale
    response_scores = jnp.einsum('ckqa,nka->kqcn', query_matrix, response_keys) * score_scale
    position = jnp.arange(RMAX)
    causal = position[:, None] >= position[None, :]
    response_scores = jnp.where(causal, response_scores, -jnp.inf)
    top = jnp.maximum(lax.optimization_barrier(jnp.max(prompt_scores, -1)), lax.optimization_barrier(jnp.max(response_scores, -1)))
    prompt_exp = jnp.exp(prompt_scores - top[..., None])
    own_exp = jnp.exp(response_scores - top[..., None])
    total = lax.optimization_barrier(jnp.sum(prompt_exp, -1)) + lax.optimization_barrier(jnp.sum(own_exp, -1))
    valid = (position < live).astype(jnp.float32)
    factor = valid / total
    prompt_w = prompt_exp * factor[..., None]
    own_w = own_exp * factor[..., None]
    prompt_weight_bwd = rounded(prompt_w)
    response_weight_bwd = rounded(own_w)
    attended_output = jnp.einsum('sixn,nsu->sixu', prompt_weight_bwd, prompt_values) + jnp.einsum('brkq,qbx->brkx', response_weight_bwd, response_values)
    delta = lax.optimization_barrier(jnp.sum(jnp.transpose(gradient_list, (1, 2, 0, 3)) * attended_output, -1))
    prompt_dp = jnp.einsum('lhgd,phd->hglp', gradient_list, prompt_values)
    response_weight_gradient = jnp.einsum('ckqa,nka->kqcn', gradient_list, response_values)
    prompt_score_gradient = rounded(prompt_w * (prompt_dp - delta[..., None]) * score_scale)
    response_score_gradient = rounded(own_w * (response_weight_gradient - delta[..., None]) * score_scale)
    query_gradient = jnp.einsum('vtcn,nva->cvta', prompt_score_gradient, prompt_keys) + jnp.einsum('zupe,ezn->pzun', response_score_gradient, response_keys)
    response_key_gradient = jnp.einsum('obes,eobp->sop', response_score_gradient, query_matrix)
    response_value_gradient = jnp.einsum('obes,eobp->sop', response_weight_bwd, gradient_list)
    prompt_dk = jnp.einsum('hglp,lhgd->phd', prompt_score_gradient, query_matrix)
    prompt_dv = jnp.einsum('hglp,lhgd->phd', prompt_weight_bwd, gradient_list)
    return (query_gradient, response_key_gradient, response_value_gradient, prompt_dk, prompt_dv)

def reference(query, resp_kv, grad_out, prefix_kv, lengths, order):
    live_all = lengths[order].astype(jnp.int32)
    prompt = prefix_kv.astype(jnp.float32).reshape(PROMPT, KVH, 2, HD)
    prompt_keys = prompt[:, :, 0]
    prompt_values = prompt[:, :, 1]

    def step(carry, inputs):
        query_rows, kv_rows, grad_rows, live = inputs
        query_matrix = query_rows.astype(jnp.float32).reshape(RMAX, KVH, GROUP, HD)
        gradient_list = grad_rows.astype(jnp.float32).reshape(RMAX, KVH, GROUP, HD)
        kv_full = kv_rows.astype(jnp.float32).reshape(RMAX, KVH, 2, HD)
        query_gradient, response_key_gradient, response_value_gradient, prompt_dk, prompt_dv = response_grads(query_matrix, kv_full, gradient_list, live, prompt_keys, prompt_values)
        d_own = jnp.stack([response_key_gradient, response_value_gradient], 2).reshape(RMAX, KVH * 2 * HD).astype(jnp.bfloat16)
        d_rows = query_gradient.reshape(RMAX, QH * HD).astype(jnp.bfloat16)
        return ((carry[0] + prompt_dk, carry[1] + prompt_dv), (d_rows, d_own))
    zeros = jnp.zeros((PROMPT, KVH, HD), jnp.float32)
    sums, outputs = lax.scan(step, (zeros, zeros), (query, resp_kv, grad_out, live_all))
    d_prefix = jnp.stack([sums[0], sums[1]], 2).reshape(PROMPT, KVH * 2 * HD)
    return (outputs[0], outputs[1], d_prefix)
```

```python
import functools
import math

import jax
import jax.numpy as jnp
from jax import lax
from jax.experimental import pallas as pl
from jax.experimental.pallas import tpu as pltpu
from jax.sharding import PartitionSpec as P

F32 = jnp.float32
BF16 = jnp.bfloat16
NEG = -1e30
CHUNK = 256
VMEM_LIMIT = 56 * 1024 * 1024


def nt(a, b):
    return lax.dot_general(a, b, (((1,), (1,)), ((), ())), preferred_element_type=F32)


def nn(a, b):
    return lax.dot_general(a, b, (((1,), (0,)), ((), ())), preferred_element_type=F32)


def tn(a, b):
    return lax.dot_general(a, b, (((0,), (0,)), ((), ())), preferred_element_type=F32)


def stack_heads(src, dst, width, group):
    length = src.shape[0]
    for h in range(group):
        dst[h * length:(h + 1) * length, :] = src[:, h * width:(h + 1) * width]


def forward_kernel(
    lengths, order, q_ref, g_ref, own_ref, *rest, width, group, blocks
):
    kv = rest[:blocks]
    dv = rest[blocks:2 * blocks]
    stats_ref, d_own_ref, dq_ref, s_ref, qr, gr = rest[2 * blocks:]
    length = q_ref.shape[0]
    rows = group * length
    per_block = kv[0].shape[0]
    steps = per_block // CHUNK
    scale = 1.0 / math.sqrt(width)
    rate = scale * math.log2(math.e)
    stack_heads(q_ref, qr, width, group)
    stack_heads(g_ref, gr, width, group)

    def fold(s, m, l):
        s3 = s.reshape(s.shape[0] // 8, 8, rows)
        m_new = jnp.maximum(m, jnp.max(s3, axis=0))
        p = jnp.exp2((s3 - m_new[None]) * rate)
        return m_new, l * jnp.exp2((m - m_new) * rate) + jnp.sum(p, axis=0)

    m = jnp.full((8, rows), NEG, F32)
    l = jnp.zeros((8, rows), F32)
    for b in range(blocks):
        def score(i, carry, b=b):
            keys = kv[b][pl.ds(i * CHUNK, CHUNK), :width]
            s = nt(keys, qr[...])
            s_ref[pl.ds(b * per_block + i * CHUNK, CHUNK), :] = s
            return fold(s, *carry)
        m, l = lax.fori_loop(0, steps, score, (m, l))

    own_k = own_ref[:, :width]
    own_v = own_ref[:, width:]
    slot = lax.rem(lax.broadcasted_iota(jnp.int32, (length, rows), 1), length)
    seen = lax.broadcasted_iota(jnp.int32, (length, rows), 0) <= slot
    s_own = jnp.where(seen, nt(own_k, qr[...]), NEG)
    m, l = fold(s_own, m, l)
    top = jnp.max(m, axis=0, keepdims=True)
    total = jnp.sum(l * jnp.exp2((m - top) * rate), axis=0, keepdims=True)
    live = lengths[order[0]]
    factor = jnp.where(slot[:1] < live, 1.0 / total, 0.0)

    out = jnp.zeros((width, rows), F32)
    for b in range(blocks):
        def values(i, out, b=b):
            at = pl.ds(i * CHUNK, CHUNK)
            s = s_ref[pl.ds(b * per_block + i * CHUNK, CHUNK), :]
            w = (jnp.exp2((s - top) * rate) * factor).astype(BF16)
            dv[b][at, :] = nn(w, gr[...]).astype(dv[b].dtype)
            return out + tn(kv[b][at, width:], w)
        out = lax.fori_loop(0, steps, values, out)

    w_own = jnp.exp2((s_own - top) * rate) * factor
    w_own16 = w_own.astype(BF16)
    out = out + tn(own_v, w_own16)
    delta = jnp.sum(gr[...].T.astype(F32) * out, axis=0, keepdims=True)
    dp = nt(own_v, gr[...])
    ds = (w_own * (dp - delta) * scale).astype(BF16)
    d_own_ref[:, :width] = nn(ds, qr[...]).astype(BF16)
    d_own_ref[:, width:] = nn(w_own16, gr[...]).astype(BF16)
    dq_ref[...] = tn(own_k, ds)
    stats_ref[0:1, :] = top
    stats_ref[1:2, :] = factor * scale
    stats_ref[2:3, :] = delta
    stats_ref[3:8, :] = jnp.zeros((5, rows), F32)


def backward_kernel(q_ref, g_ref, stats_ref, dq_in, *rest, width, group, blocks, last):
    kv = rest[:blocks]
    dk = rest[blocks:2 * blocks]
    dq_out, qr, gr = rest[2 * blocks:]
    length = q_ref.shape[0]
    steps = kv[0].shape[0] // CHUNK
    rate = math.log2(math.e) / math.sqrt(width)
    stack_heads(q_ref, qr, width, group)
    stack_heads(g_ref, gr, width, group)
    top = stats_ref[0:1, :]
    factor = stats_ref[1:2, :]
    delta = stats_ref[2:3, :]
    dq = dq_in[...]
    for b in range(blocks):
        def step(i, dq, b=b):
            at = pl.ds(i * CHUNK, CHUNK)
            keys = kv[b][at, :width]
            s = nt(keys, qr[...])
            dp = nt(kv[b][at, width:], gr[...])
            ds = (jnp.exp2((s - top) * rate) * factor * (dp - delta)).astype(BF16)
            dk[b][at, :] = nn(ds, qr[...]).astype(dk[b].dtype)
            return dq + tn(keys, ds)
        dq = lax.fori_loop(0, steps, step, dq)
    if last:
        for h in range(group):
            part = dq[:, h * length:(h + 1) * length]
            dq_out[:, h * width:(h + 1) * width] = part.T.astype(BF16)
    else:
        dq_out[...] = dq


VM = pl.BlockSpec(memory_space=pltpu.VMEM)
SM = pl.BlockSpec(memory_space=pltpu.SMEM)


def run_forward(lengths, order, q, g, own, kv, dv_types, width):
    length = q.shape[0]
    group = q.shape[1] // width
    rows = group * length
    per_block = kv[0].shape[0]
    prompt = per_block * len(kv)
    return pl.pallas_call(
        functools.partial(forward_kernel, width=width, group=group, blocks=len(kv)),
        out_shape=[jax.ShapeDtypeStruct((per_block, width), t) for t in dv_types]
        + [
            jax.ShapeDtypeStruct((8, rows), F32),
            jax.ShapeDtypeStruct((length, 2 * width), BF16),
            jax.ShapeDtypeStruct((width, rows), F32),
        ],
        in_specs=[SM, SM] + [VM] * (3 + len(kv)),
        out_specs=[VM] * (len(kv) + 3),
        scratch_shapes=[
            pltpu.VMEM((prompt, rows), F32),
            pltpu.VMEM((rows, width), BF16),
            pltpu.VMEM((rows, width), BF16),
        ],
        compiler_params=pltpu.CompilerParams(vmem_limit_bytes=VMEM_LIMIT),
        cost_estimate=pl.CostEstimate(
            flops=10 * prompt * rows * width, bytes_accessed=1 << 22, transcendentals=0
        ),
        name="forward",
    )(lengths, order, q, g, own, *kv)


def run_backward(q, g, stats, dq, kv, dk_types, width, last):
    length = q.shape[0]
    group = q.shape[1] // width
    rows = group * length
    per_block = kv[0].shape[0]
    prompt = per_block * len(kv)
    dq_type = (
        jax.ShapeDtypeStruct((length, group * width), BF16)
        if last
        else jax.ShapeDtypeStruct((width, rows), F32)
    )
    return pl.pallas_call(
        functools.partial(
            backward_kernel, width=width, group=group, blocks=len(kv), last=last
        ),
        out_shape=[jax.ShapeDtypeStruct((per_block, width), t) for t in dk_types] + [dq_type],
        in_specs=[VM] * (4 + len(kv)),
        out_specs=[VM] * (len(kv) + 1),
        scratch_shapes=[
            pltpu.VMEM((rows, width), BF16),
            pltpu.VMEM((rows, width), BF16),
        ],
        compiler_params=pltpu.CompilerParams(vmem_limit_bytes=VMEM_LIMIT),
        cost_estimate=pl.CostEstimate(
            flops=14 * prompt * rows * width, bytes_accessed=1 << 22, transcendentals=0
        ),
        name="backward",
    )(q, g, stats, dq, *kv)


def per_device(query, resp_kv, grad_out, prefix_kv, lengths, order, *, layers):
    width = resp_kv.shape[2] // 2
    shard = prefix_kv.shape[0]
    q, g, own = query[0], grad_out[0], resp_kv[0]
    to_core = [(i, i ^ 1) for i in range(4 * layers)]
    to_x = [(i, i ^ 2) for i in range(4 * layers)]
    rings = [[4 * z + i for z in range(layers)] for i in range(4)]

    kv_mine = lax.all_gather(prefix_kv, "roll", axis=0, tiled=True, axis_index_groups=rings)
    kv_x = lax.ppermute(kv_mine, "roll", to_x)
    kv_core = lax.ppermute(kv_mine, "roll", to_core)
    kv_diag = lax.ppermute(kv_x, "roll", to_core)

    dv_core, dv_diag, dv_x, dv_mine, stats, d_own, dq = run_forward(
        lengths, order, q, g, own, [kv_core, kv_diag, kv_x, kv_mine],
        [BF16, BF16, F32, F32], width,
    )
    parts = d_own.reshape(8, d_own.shape[0] // 8, 2 * width)
    parts = lax.all_to_all(parts, "head", split_axis=0, concat_axis=0, tiled=True)
    d_resp = jnp.transpose(parts, (1, 0, 2)).reshape(1, parts.shape[1], -1)

    dk_core, dk_diag, dq = run_backward(
        q, g, stats, dq, [kv_core, kv_diag], [BF16, BF16], width, False
    )
    dk_x, dk_mine, d_query = run_backward(
        q, g, stats, dq, [kv_x, kv_mine], [F32, F32], width, True
    )

    def collect(core, diag, x, mine):
        got_mine = lax.ppermute(core, "roll", to_core)
        got_x = lax.ppermute(diag, "roll", to_core)
        over = lax.ppermute((x + got_x).astype(BF16), "roll", to_x)
        term = (mine + got_mine + over).astype(BF16).reshape(layers, shard, width)
        terms = lax.all_to_all(
            term, "roll", split_axis=0, concat_axis=0, tiled=True, axis_index_groups=rings
        )
        return jnp.sum(terms.astype(F32), axis=0)

    values = collect(dv_core, dv_diag, dv_x, dv_mine)
    keys = collect(dk_core, dk_diag, dk_x, dk_mine)
    return d_query[None], d_resp, jnp.concatenate([keys, values], axis=1)


def solution(mesh):
    layers = mesh.shape["roll"] // 4
    return jax.shard_map(
        functools.partial(per_device, layers=layers),
        mesh=mesh,
        in_specs=(
            P("roll", None, "head"),
            P("roll", None, "head"),
            P("roll", None, "head"),
            P("roll", "head"),
            P(),
            P("roll"),
        ),
        out_specs=(P("roll", None, "head"), P("roll", "head", None), P("roll", "head")),
        check_vma=False,
    )
```

```python
import functools
import math

import jax
import jax.numpy as jnp
from jax import lax
from jax.experimental import pallas as pl
from jax.experimental.pallas import tpu as pltpu
from jax.sharding import PartitionSpec as P

F32 = jnp.float32
BF16 = jnp.bfloat16
NEG = -1e30
CHUNK = 256
VMEM_LIMIT = 56 * 1024 * 1024


def nt(a, b):
    return lax.dot_general(a, b, (((1,), (1,)), ((), ())), preferred_element_type=F32)


def nn(a, b):
    return lax.dot_general(a, b, (((1,), (0,)), ((), ())), preferred_element_type=F32)


def tn(a, b):
    return lax.dot_general(a, b, (((0,), (0,)), ((), ())), preferred_element_type=F32)


def stack_heads(src, dst, width, group):
    length = src.shape[0]
    for h in range(group):
        dst[h * length:(h + 1) * length, :] = src[:, h * width:(h + 1) * width]


def attention_kernel(
    lengths, order, q_ref, g_ref, own_ref, mine, other,
    send_ref, keep_ref, d_own_ref, dq_ref, p_ref, qr, gr, *, width, group,
):
    length = q_ref.shape[0]
    rows = group * length
    count = mine.shape[0]
    scale = 1.0 / math.sqrt(width)
    rate = scale * math.log2(math.e)
    stack_heads(q_ref, qr, width, group)
    stack_heads(g_ref, gr, width, group)

    tiles = []
    for side, (kv, grads) in enumerate(((other, send_ref), (mine, keep_ref))):
        for at in range(0, count, CHUNK):
            here = pl.ds(at, CHUNK)
            k, v = kv.at[here, pl.ds(0, width)], kv.at[here, pl.ds(width, width)]
            tiles.append((pl.ds(side * count + at, CHUNK), k, v, grads, here))

    def eights(a):
        return a.reshape(a.shape[0] // 8, 8, rows)

    own_k = own_ref[:, :width]
    own_v = own_ref[:, width:]
    slot = lax.rem(lax.broadcasted_iota(jnp.int32, (length, rows), 1), length)
    seen = lax.broadcasted_iota(jnp.int32, (length, rows), 0) <= slot
    s_own = jnp.where(seen, nt(own_k, qr[...]), NEG)
    m = jnp.max(eights(s_own), axis=0)
    for at, k, v, grads, here in tiles:
        s = nt(k[...], qr[...])
        p_ref[at, :] = s
        m = jnp.maximum(m, jnp.max(eights(s), axis=0))
    top = jnp.max(m, axis=0, keepdims=True)

    p_own = jnp.exp2((s_own - top) * rate)
    l = jnp.sum(eights(p_own), axis=0)
    for at, k, v, grads, here in tiles:
        p = jnp.exp2((p_ref[at, :] - top) * rate)
        p_ref[at, :] = p
        l = l + jnp.sum(eights(p), axis=0)
    total = jnp.sum(l, axis=0, keepdims=True)
    live = lengths[order[0]]
    factor = jnp.where(slot[:1] < live, 1.0 / total, 0.0)

    w_own = p_own * factor
    w_own16 = w_own.astype(BF16)
    out = tn(own_v, w_own16)
    for at, k, v, grads, here in tiles:
        w = (p_ref[at, :] * factor).astype(BF16)
        grads[here, width:] = nn(w, gr[...]).astype(grads.dtype)
        out = out + tn(v[...], w)
    delta = jnp.sum(gr[...].T.astype(F32) * out, axis=0, keepdims=True)

    ds_own = (w_own * (nt(own_v, gr[...]) - delta) * scale).astype(BF16)
    d_own_ref[:, :width] = nn(ds_own, qr[...]).astype(BF16)
    d_own_ref[:, width:] = nn(w_own16, gr[...]).astype(BF16)
    dq = tn(own_k, ds_own)
    factor = factor * scale
    for at, k, v, grads, here in tiles:
        ds = (p_ref[at, :] * factor * (nt(v[...], gr[...]) - delta)).astype(BF16)
        grads[here, :width] = nn(ds, qr[...]).astype(grads.dtype)
        dq = dq + tn(k[...], ds)
    for h in range(group):
        part_h = dq[:, h * length:(h + 1) * length]
        dq_ref[:, h * width:(h + 1) * width] = part_h.T.astype(BF16)


VM = pl.BlockSpec(memory_space=pltpu.VMEM)
SM = pl.BlockSpec(memory_space=pltpu.SMEM)


def run_attention(lengths, order, q, g, own, mine, other, width):
    length = q.shape[0]
    group = q.shape[1] // width
    rows = group * length
    count = mine.shape[0]
    return pl.pallas_call(
        functools.partial(attention_kernel, width=width, group=group),
        out_shape=[
            jax.ShapeDtypeStruct((count, 2 * width), BF16),
            jax.ShapeDtypeStruct((count, 2 * width), F32),
            jax.ShapeDtypeStruct((length, 2 * width), BF16),
            jax.ShapeDtypeStruct((length, group * width), BF16),
        ],
        in_specs=[SM, SM] + [VM] * 5,
        out_specs=[VM] * 4,
        scratch_shapes=[
            pltpu.VMEM((2 * count, rows), F32),
            pltpu.VMEM((rows, width), BF16),
            pltpu.VMEM((rows, width), BF16),
        ],
        compiler_params=pltpu.CompilerParams(vmem_limit_bytes=VMEM_LIMIT),
        cost_estimate=pl.CostEstimate(
            flops=24 * count * rows * width, bytes_accessed=1 << 23, transcendentals=0
        ),
        name="attention",
    )(lengths, order, q, g, own, mine, other)


def per_device(query, resp_kv, grad_out, prefix_kv, lengths, order, *, layers, heads):
    width = resp_kv.shape[2] // 2
    shard = prefix_kv.shape[0]
    q, g, own = query[0], grad_out[0], resp_kv[0]
    far = layers // 2
    to_core = [(i, i ^ 1) for i in range(4 * layers)]
    rings = [[4 * (2 * b + a) + i for b in range(far)] for a in range(2) for i in range(4)]
    squares = [[8 * b + 4 * a + 2 * x + c for a in range(2) for x in range(2)] for b in range(far) for c in range(2)]

    def exchange(array, groups):
        return lax.all_to_all(
            array, "roll", split_axis=0, concat_axis=0, tiled=True, axis_index_groups=groups
        )

    def to_all(array, groups):
        copies = len(groups[0])
        sent = jnp.broadcast_to(array[None], (copies,) + array.shape)
        return exchange(sent, groups).reshape(copies * array.shape[0], array.shape[1])

    def total(terms, groups):
        terms = terms.astype(BF16).reshape(len(groups[0]), -1, terms.shape[1])
        return jnp.sum(exchange(terms, groups).astype(F32), axis=0)

    mine = to_all(to_all(prefix_kv, rings), squares)
    other = lax.ppermute(mine, "roll", to_core)

    send, keep, d_own, d_query = run_attention(lengths, order, q, g, own, mine, other, width)
    parts = d_own.reshape(heads, -1, 2 * width)
    parts = lax.all_to_all(parts, "head", split_axis=0, concat_axis=0, tiled=True)
    got = lax.ppermute(send, "roll", to_core)
    terms = (keep + got).astype(BF16)
    terms, parts = lax.optimization_barrier((terms, parts))
    d_resp = jnp.transpose(parts, (1, 0, 2)).reshape(1, parts.shape[1], -1)
    terms = total(terms, squares).astype(BF16)
    return d_query[None], d_resp, total(terms, rings)


def solution(mesh):
    layers = mesh.shape["roll"] // 4
    return jax.shard_map(
        functools.partial(per_device, layers=layers, heads=mesh.shape["head"]),
        mesh=mesh,
        in_specs=(
            P("roll", None, "head"),
            P("roll", None, "head"),
            P("roll", None, "head"),
            P("roll", "head"),
            P(),
            P("roll"),
        ),
        out_specs=(P("roll", None, "head"), P("roll", "head", None), P("roll", "head")),
        check_vma=False,
    )
```

```python
import functools
import math

import jax
import jax.numpy as jnp
from jax import lax
from jax.experimental import pallas as pl
from jax.experimental.pallas import tpu as pltpu
from jax.sharding import PartitionSpec as P

F32 = jnp.float32
BF16 = jnp.bfloat16
NEG = -1e30
CHUNK = 512
VMEM_LIMIT = 32 * 1024 * 1024


def nt(a, b):
    return lax.dot_general(a, b, (((1,), (1,)), ((), ())), preferred_element_type=F32)


def nn(a, b):
    return lax.dot_general(a, b, (((1,), (0,)), ((), ())), preferred_element_type=F32)


def tn(a, b):
    return lax.dot_general(a, b, (((0,), (0,)), ((), ())), preferred_element_type=F32)


def stack_heads(src, dst, width, group):
    length = src.shape[0]
    for h in range(group):
        dst[h * length:(h + 1) * length, :] = src[:, h * width:(h + 1) * width]


def attention_kernel(
    lengths, order, head, q_ref, g_ref, own_ref, mine, other,
    send_ref, keep_ref, d_own_ref, dq_ref, p_ref, qr, gr, d_own, *, width, group,
):
    length = q_ref.shape[0]
    rows = group * length
    count = mine.shape[0]
    scale = 1.0 / math.sqrt(width)
    rate = scale * math.log2(math.e)
    stack_heads(q_ref, qr, width, group)
    stack_heads(g_ref, gr, width, group)

    tiles = []
    for side, (kv, grads) in enumerate(((other, send_ref), (mine, keep_ref))):
        for at in range(0, count, CHUNK):
            here = pl.ds(at, CHUNK)
            k, v = kv.at[here, pl.ds(0, width)], kv.at[here, pl.ds(width, width)]
            tiles.append((pl.ds(side * count + at, CHUNK), k, v, grads, here))

    def eights(a):
        return a.reshape(a.shape[0] // 8, 8, rows)

    own_k = own_ref[:, :width]
    own_v = own_ref[:, width:]
    slot = lax.rem(lax.broadcasted_iota(jnp.int32, (length, rows), 1), length)
    seen = lax.broadcasted_iota(jnp.int32, (length, rows), 0) <= slot
    s_own = jnp.where(seen, nt(own_k, qr[...]), NEG)
    m = jnp.max(eights(s_own), axis=0)
    for at, k, v, grads, here in tiles:
        s = nt(k[...], qr[...])
        p_ref[at, :] = s
        m = jnp.maximum(m, jnp.max(eights(s), axis=0))
    top = jnp.max(m, axis=0, keepdims=True)

    p_own = jnp.exp2((s_own - top) * rate)
    l = jnp.sum(eights(p_own), axis=0)
    for at, k, v, grads, here in tiles:
        p = jnp.exp2((p_ref[at, :] - top) * rate)
        p_ref[at, :] = p
        l = l + jnp.sum(eights(p), axis=0)
    total = jnp.sum(l, axis=0, keepdims=True)
    live = lengths[order[0]]
    factor = jnp.where(slot[:1] < live, 1.0 / total, 0.0)

    w_own = p_own * factor
    w_own16 = w_own.astype(BF16)
    out = tn(own_v, w_own16)
    for at, k, v, grads, here in tiles:
        w = (p_ref[at, :] * factor).astype(BF16)
        grads[here, width:] = nn(w, gr[...]).astype(grads.dtype)
        out = out + tn(v[...], w)
    delta = jnp.sum(gr[...].T.astype(F32) * out, axis=0, keepdims=True)

    ds_own = (w_own * (nt(own_v, gr[...]) - delta) * scale).astype(BF16)
    d_own[:, :width] = nn(ds_own, qr[...]).astype(BF16)
    d_own[:, width:] = nn(w_own16, gr[...]).astype(BF16)
    heads, slots = d_own_ref.shape[:2]
    for i in range(heads):
        at = pl.multiple_of((head[0] ^ i) * slots, slots)
        d_own_ref[i] = d_own[pl.ds(at, slots), :]
    dq = tn(own_k, ds_own)
    factor = factor * scale
    for at, k, v, grads, here in tiles:
        ds = (p_ref[at, :] * factor * (nt(v[...], gr[...]) - delta)).astype(BF16)
        grads[here, :width] = nn(ds, qr[...]).astype(grads.dtype)
        dq = dq + tn(k[...], ds)
    for h in range(group):
        part_h = dq[:, h * length:(h + 1) * length]
        dq_ref[:, h * width:(h + 1) * width] = part_h.T.astype(BF16)


VM = pl.BlockSpec(memory_space=pltpu.VMEM)
SM = pl.BlockSpec(memory_space=pltpu.SMEM)


def run_attention(lengths, order, head, heads, q, g, own, mine, other, width):
    length = q.shape[0]
    group = q.shape[1] // width
    rows = group * length
    count = mine.shape[0]
    return pl.pallas_call(
        functools.partial(attention_kernel, width=width, group=group),
        out_shape=[
            jax.ShapeDtypeStruct((count, 2 * width), BF16),
            jax.ShapeDtypeStruct((count, 2 * width), F32),
            jax.ShapeDtypeStruct((heads, length // heads, 2 * width), BF16),
            jax.ShapeDtypeStruct((length, group * width), BF16),
        ],
        in_specs=[SM, SM, SM] + [VM] * 5,
        out_specs=[VM] * 4,
        scratch_shapes=[
            pltpu.VMEM((2 * count, rows), F32),
            pltpu.VMEM((rows, width), BF16),
            pltpu.VMEM((rows, width), BF16),
            pltpu.VMEM((length, 2 * width), BF16),
        ],
        compiler_params=pltpu.CompilerParams(vmem_limit_bytes=VMEM_LIMIT),
        cost_estimate=pl.CostEstimate(
            flops=24 * count * rows * width, bytes_accessed=1 << 23, transcendentals=0
        ),
        name="attention",
    )(lengths, order, head, q, g, own, mine, other)


def per_device(query, resp_kv, grad_out, prefix_kv, lengths, order, *, layers, heads):
    width = resp_kv.shape[2] // 2
    shard = prefix_kv.shape[0]
    q, g, own = query[0], grad_out[0], resp_kv[0]
    far = layers // 2
    to_core = [(i, i ^ 1) for i in range(4 * layers)]
    rings = [[4 * (2 * b + a) + i for b in range(far)] for a in range(2) for i in range(4)]
    squares = [[8 * b + 4 * a + 2 * x + c for a in range(2) for x in range(2)] for b in range(far) for c in range(2)]

    def exchange(array, groups):
        return lax.all_to_all(
            array, "roll", split_axis=0, concat_axis=0, tiled=True, axis_index_groups=groups
        )

    def to_all(array, groups):
        copies = len(groups[0])
        sent = jnp.broadcast_to(array[None], (copies,) + array.shape)
        return exchange(sent, groups).reshape(copies * array.shape[0], array.shape[1])

    def total(terms, groups):
        terms = terms.astype(BF16).reshape(len(groups[0]), -1, terms.shape[1])
        return jnp.sum(exchange(terms, groups).astype(F32), axis=0)

    mine = to_all(to_all(prefix_kv, rings), squares)
    other = lax.ppermute(mine, "roll", to_core)

    head = lax.axis_index("head").astype(jnp.int32)
    send, keep, d_own, d_query = run_attention(
        lengths, order, head.reshape(1), heads, q, g, own, mine, other, width
    )
    got = lax.ppermute(send, "roll", to_core)
    terms = (keep + got).astype(BF16)
    terms, d_own = lax.optimization_barrier((terms, d_own))

    def swap_heads(blocks, bit):
        sent = [i for i in range(heads) if i & bit]
        swapped = lax.ppermute(
            jnp.stack([blocks[i] for i in sent]), "head", [(i, i ^ bit) for i in range(heads)]
        )
        return [swapped[sent.index(i)] if i & bit else blocks[i] for i in range(heads)]

    blocks = [d_own[i] for i in range(heads)]
    bits = [1 << i for i in range(heads.bit_length() - 1)]
    for bit in bits[:-1]:
        blocks = swap_heads(blocks, bit)
    terms = total(terms, squares).astype(BF16)
    terms, blocks = lax.optimization_barrier((terms, blocks))
    blocks = swap_heads(blocks, bits[-1])
    d_prefix = total(terms, rings)

    for bit in bits:
        odd = (head & bit) != 0
        blocks = [jnp.where(odd, blocks[i ^ bit], blocks[i]) for i in range(heads)]
    d_resp = jnp.concatenate(blocks, axis=1)
    return d_query[None], d_resp[None], d_prefix


def solution(mesh):
    layers = mesh.shape["roll"] // 4
    return jax.shard_map(
        functools.partial(per_device, layers=layers, heads=mesh.shape["head"]),
        mesh=mesh,
        in_specs=(
            P("roll", None, "head"),
            P("roll", None, "head"),
            P("roll", None, "head"),
            P("roll", "head"),
            P(),
            P("roll"),
        ),
        out_specs=(P("roll", None, "head"), P("roll", "head", None), P("roll", "head")),
        check_vma=False,
    )
```

```python
import functools
import math

import jax
import jax.numpy as jnp
from jax import lax
from jax.experimental import pallas as pl
from jax.experimental.pallas import tpu as pltpu
from jax.sharding import PartitionSpec as P

F32 = jnp.float32
BF16 = jnp.bfloat16
NEG = -1e30
CHUNK = 512
VMEM_LIMIT = 32 * 1024 * 1024


def nt(a, b):
    return lax.dot_general(a, b, (((1,), (1,)), ((), ())), preferred_element_type=F32)


def nn(a, b):
    return lax.dot_general(a, b, (((1,), (0,)), ((), ())), preferred_element_type=F32)


def tn(a, b):
    return lax.dot_general(a, b, (((0,), (0,)), ((), ())), preferred_element_type=F32)


def attention_kernel(
    lengths, order, head, qr, gr, own_ref, mine, other,
    send_ref, keep_ref, d_own_ref, dq_ref, p_ref, d_own, *, width, group,
):
    rows = qr.shape[0]
    length = rows // group
    count = mine.shape[0]
    scale = 1.0 / math.sqrt(width)
    rate = scale * math.log2(math.e)
    tiles = []
    for side, (kv, grads) in enumerate(((other, send_ref), (mine, keep_ref))):
        for at in range(0, count, CHUNK):
            here = pl.ds(at, CHUNK)
            k, v = kv.at[here, pl.ds(0, width)], kv.at[here, pl.ds(width, width)]
            tiles.append((pl.ds(side * count + at, CHUNK), k, v, grads, here))

    def eights(a):
        return a.reshape(a.shape[0] // 8, 8, rows)

    own_k = own_ref[:, :width]
    own_v = own_ref[:, width:]
    slot = lax.rem(lax.broadcasted_iota(jnp.int32, (length, rows), 1), length)
    seen = lax.broadcasted_iota(jnp.int32, (length, rows), 0) <= slot
    s_own = jnp.where(seen, nt(own_k, qr[...]), NEG)
    m = jnp.max(eights(s_own), axis=0)
    for at, k, v, grads, here in tiles:
        s = nt(k[...], qr[...])
        p_ref[at, :] = s
        m = jnp.maximum(m, jnp.max(eights(s), axis=0))
    top = jnp.max(m, axis=0, keepdims=True)

    p_own = jnp.exp2((s_own - top) * rate)
    l = jnp.sum(eights(p_own), axis=0)
    for at, k, v, grads, here in tiles:
        p = jnp.exp2((p_ref[at, :] - top) * rate)
        p_ref[at, :] = p
        l = l + jnp.sum(eights(p), axis=0)
    total = jnp.sum(l, axis=0, keepdims=True)
    live = lengths[order[0]]
    factor = jnp.where(slot[:1] < live, 1.0 / total, 0.0)

    w_own = p_own * factor
    w_own16 = w_own.astype(BF16)
    out = tn(own_v, w_own16)
    for at, k, v, grads, here in tiles:
        w = (p_ref[at, :] * factor).astype(BF16)
        grads[here, width:] = nn(w, gr[...]).astype(grads.dtype)
        out = out + tn(v[...], w)
    delta = jnp.sum(gr[...].T.astype(F32) * out, axis=0, keepdims=True)

    ds_own = (w_own * (nt(own_v, gr[...]) - delta) * scale).astype(BF16)
    d_own[:, :width] = nn(ds_own, qr[...]).astype(BF16)
    d_own[:, width:] = nn(w_own16, gr[...]).astype(BF16)
    heads, slots = d_own_ref.shape[:2]
    for i in range(heads):
        at = pl.multiple_of((head[0] ^ i) * slots, slots)
        d_own_ref[i] = d_own[pl.ds(at, slots), :]
    dq = tn(own_k, ds_own)
    factor = factor * scale
    for at, k, v, grads, here in tiles:
        ds = (p_ref[at, :] * factor * (nt(v[...], gr[...]) - delta)).astype(BF16)
        grads[here, :width] = nn(ds, qr[...]).astype(grads.dtype)
        dq = dq + tn(k[...], ds)
    for h in range(group):
        part_h = dq[:, h * length:(h + 1) * length]
        dq_ref[:, h * width:(h + 1) * width] = part_h.T.astype(BF16)


VM = pl.BlockSpec(memory_space=pltpu.VMEM)
SM = pl.BlockSpec(memory_space=pltpu.SMEM)


def run_attention(lengths, order, head, heads, q, g, own, mine, other, width):
    rows = q.shape[0]
    length = own.shape[0]
    group = rows // length
    count = mine.shape[0]
    return pl.pallas_call(
        functools.partial(attention_kernel, width=width, group=group),
        out_shape=[
            jax.ShapeDtypeStruct((count, 2 * width), BF16),
            jax.ShapeDtypeStruct((count, 2 * width), F32),
            jax.ShapeDtypeStruct((heads, length // heads, 2 * width), BF16),
            jax.ShapeDtypeStruct((length, group * width), BF16),
        ],
        in_specs=[SM, SM, SM] + [VM] * 5,
        out_specs=[VM] * 4,
        scratch_shapes=[
            pltpu.VMEM((2 * count, rows), F32),
            pltpu.VMEM((length, 2 * width), BF16),
        ],
        compiler_params=pltpu.CompilerParams(vmem_limit_bytes=VMEM_LIMIT),
        cost_estimate=pl.CostEstimate(
            flops=24 * count * rows * width, bytes_accessed=1 << 23, transcendentals=0
        ),
        name="attention",
    )(lengths, order, head, q, g, own, mine, other)


def per_device(query, resp_kv, grad_out, prefix_kv, lengths, order, *, layers, heads):
    width = resp_kv.shape[2] // 2
    shard = prefix_kv.shape[0]
    own = resp_kv[0]
    length = own.shape[0]

    def stack_heads(a):
        return jnp.transpose(a[0].reshape(length, -1, width), (1, 0, 2)).reshape(-1, width)

    q, g = stack_heads(query), stack_heads(grad_out)
    far = layers // 2
    to_core = [(i, i ^ 1) for i in range(4 * layers)]
    rings = [[4 * (2 * b + a) + i for b in range(far)] for a in range(2) for i in range(4)]
    squares = [[8 * b + 4 * a + 2 * x + c for a in range(2) for x in range(2)] for b in range(far) for c in range(2)]

    def exchange(array, groups):
        return lax.all_to_all(
            array, "roll", split_axis=0, concat_axis=0, tiled=True, axis_index_groups=groups
        )

    def to_all(array, groups):
        copies = len(groups[0])
        sent = jnp.broadcast_to(array[None], (copies,) + array.shape)
        return exchange(sent, groups).reshape(copies * array.shape[0], array.shape[1])

    def terms_of_all(terms, groups):
        return exchange(terms.astype(BF16).reshape(len(groups[0]), -1, terms.shape[1]), groups)

    def total(terms):
        return jnp.sum(terms.astype(F32), axis=0)

    mine = to_all(to_all(prefix_kv, rings), squares)
    other = lax.ppermute(mine, "roll", to_core)

    head = lax.axis_index("head").astype(jnp.int32)
    send, keep, d_own, d_query = run_attention(
        lengths, order, head.reshape(1), heads, q, g, own, mine, other, width
    )
    got = lax.ppermute(send, "roll", to_core)
    terms = (keep + got).astype(BF16)
    terms, d_own = lax.optimization_barrier((terms, d_own))

    def swap_heads(blocks, bit):
        sent = [i for i in range(heads) if i & bit]
        swapped = lax.ppermute(
            jnp.stack([blocks[i] for i in sent]), "head", [(i, i ^ bit) for i in range(heads)]
        )
        return [swapped[sent.index(i)] if i & bit else blocks[i] for i in range(heads)]

    blocks = [d_own[i] for i in range(heads)]
    bits = [1 << i for i in range(heads.bit_length() - 1)]
    for bit in bits[:-1]:
        blocks = swap_heads(blocks, bit)
    terms = total(terms_of_all(terms, squares)).astype(BF16)
    terms, blocks = lax.optimization_barrier((terms, blocks))
    blocks = swap_heads(blocks, bits[-1])
    terms = terms_of_all(terms, rings)
    terms, blocks = lax.optimization_barrier((terms, blocks))
    d_prefix = total(terms)

    for bit in bits:
        odd = (head & bit) != 0
        blocks = [jnp.where(odd, blocks[i ^ bit], blocks[i]) for i in range(heads)]
    d_resp = jnp.concatenate(blocks, axis=1)
    return d_query[None], d_resp[None], d_prefix


def solution(mesh):
    layers = mesh.shape["roll"] // 4
    return jax.shard_map(
        functools.partial(per_device, layers=layers, heads=mesh.shape["head"]),
        mesh=mesh,
        in_specs=(
            P("roll", None, "head"),
            P("roll", None, "head"),
            P("roll", None, "head"),
            P("roll", "head"),
            P(),
            P("roll"),
        ),
        out_specs=(P("roll", None, "head"), P("roll", "head", None), P("roll", "head")),
        check_vma=False,
    )
```

```python
import functools
import math

import jax
import jax.numpy as jnp
from jax import lax
from jax.experimental import pallas as pl
from jax.experimental.pallas import tpu as pltpu
from jax.sharding import PartitionSpec as P

F32 = jnp.float32
BF16 = jnp.bfloat16
NEG = -1e30
CHUNK = 512
VMEM_LIMIT = 32 * 1024 * 1024


def nt(a, b):
    return lax.dot_general(a, b, (((1,), (1,)), ((), ())), preferred_element_type=F32)


def nn(a, b):
    return lax.dot_general(a, b, (((1,), (0,)), ((), ())), preferred_element_type=F32)


def tn(a, b):
    return lax.dot_general(a, b, (((0,), (0,)), ((), ())), preferred_element_type=F32)


def attention_kernel(
    lengths, order, head, qr, gr, own_ref, mine, other,
    send_ref, keep_ref, d_own_ref, dq_ref, rest_ref, p_mine, p_other, d_own, *, width, group,
):
    rows = qr.shape[0]
    length = rows // group
    count = mine.shape[0]
    scale = 1.0 / math.sqrt(width)
    rate = scale * math.log2(math.e)
    tiles = []
    for side, (kv, grads) in enumerate(((other, send_ref), (mine, keep_ref))):
        for at in range(0, count, CHUNK):
            here = pl.ds(at, CHUNK)
            k, v = kv.at[here, pl.ds(0, width)], kv.at[here, pl.ds(width, width)]
            tiles.append(((p_other, p_mine)[side], here, k, v, grads))

    def eights(a):
        return a.reshape(a.shape[0] // 8, 8, rows)

    own_k = own_ref[:, :width]
    own_v = own_ref[:, width:]
    slot = lax.rem(lax.broadcasted_iota(jnp.int32, (length, rows), 1), length)
    seen = lax.broadcasted_iota(jnp.int32, (length, rows), 0) <= slot
    s_own = jnp.where(seen, nt(own_k, qr[...]), NEG)
    m = jnp.max(eights(s_own), axis=0)
    for p_ref, at, k, v, grads in tiles:
        s = nt(k[...], qr[...])
        p_ref[at, :] = s
        m = jnp.maximum(m, jnp.max(eights(s), axis=0))
    top = jnp.max(m, axis=0, keepdims=True)

    p_own = jnp.exp2((s_own - top) * rate)
    l = jnp.sum(eights(p_own), axis=0)
    for p_ref, at, k, v, grads in tiles:
        p = jnp.exp2((p_ref[at, :] - top) * rate)
        p_ref[at, :] = p
        l = l + jnp.sum(eights(p), axis=0)
    total = jnp.sum(l, axis=0, keepdims=True)
    live = lengths[order[0]]
    factor = jnp.where(slot[:1] < live, 1.0 / total, 0.0)

    w_own = p_own * factor
    w_own16 = w_own.astype(BF16)
    out = tn(own_v, w_own16)
    for p_ref, at, k, v, grads in tiles:
        w = (p_ref[at, :] * factor).astype(BF16)
        if grads is send_ref:
            grads[at, width:] = nn(w, gr[...]).astype(grads.dtype)
        else:
            grads[at, :] = nn(w, gr[...])
        out = out + tn(v[...], w)
    delta = jnp.sum(gr[...].T.astype(F32) * out, axis=0, keepdims=True)

    ds_own = (w_own * (nt(own_v, gr[...]) - delta) * scale).astype(BF16)
    d_own[:, :width] = nn(ds_own, qr[...]).astype(BF16)
    d_own[:, width:] = nn(w_own16, gr[...]).astype(BF16)
    heads, slots = d_own_ref.shape[:2]
    for i in range(heads):
        at = pl.multiple_of((head[0] ^ i) * slots, slots)
        d_own_ref[i] = d_own[pl.ds(at, slots), :]
    dq = tn(own_k, ds_own)
    factor = factor * scale
    for p_ref, at, k, v, grads in tiles[:len(tiles) // 2]:
        ds = (p_ref[at, :] * factor * (nt(v[...], gr[...]) - delta)).astype(BF16)
        grads[at, :width] = nn(ds, qr[...]).astype(grads.dtype)
        dq = dq + tn(k[...], ds)
    dq_ref[...] = dq
    rest_ref[0:1, :] = factor
    rest_ref[1:2, :] = delta
    rest_ref[2:8, :] = jnp.zeros((6, rows), F32)


def own_slopes_kernel(qr, gr, mine, p_mine, rest, dq_in, dk_ref, dq_ref, *, width, group):
    length = qr.shape[0] // group
    factor, delta = rest[0:1, :], rest[1:2, :]
    dq = dq_in[...]
    for start in range(0, mine.shape[0], CHUNK):
        at = pl.ds(start, CHUNK)
        ds = (p_mine[at, :] * factor * (nt(mine[at, width:], gr[...]) - delta)).astype(BF16)
        dk_ref[at, :] = nn(ds, qr[...])
        dq = dq + tn(mine[at, :width], ds)
    for h in range(group):
        part_h = dq[:, h * length:(h + 1) * length]
        dq_ref[:, h * width:(h + 1) * width] = part_h.T.astype(BF16)


VM = pl.BlockSpec(memory_space=pltpu.VMEM)
SM = pl.BlockSpec(memory_space=pltpu.SMEM)


def run_attention(lengths, order, head, heads, q, g, own, mine, other, width):
    rows = q.shape[0]
    length = own.shape[0]
    group = rows // length
    count = mine.shape[0]
    params = pltpu.CompilerParams(vmem_limit_bytes=VMEM_LIMIT)
    send, dv, d_own, dq, rest, p_mine = pl.pallas_call(
        functools.partial(attention_kernel, width=width, group=group),
        out_shape=[
            jax.ShapeDtypeStruct((count, 2 * width), BF16),
            jax.ShapeDtypeStruct((count, width), F32),
            jax.ShapeDtypeStruct((heads, length // heads, 2 * width), BF16),
            jax.ShapeDtypeStruct((width, rows), F32),
            jax.ShapeDtypeStruct((8, rows), F32),
            jax.ShapeDtypeStruct((count, rows), F32),
        ],
        in_specs=[SM, SM, SM] + [VM] * 5,
        out_specs=[VM] * 6,
        scratch_shapes=[
            pltpu.VMEM((count, rows), F32),
            pltpu.VMEM((length, 2 * width), BF16),
        ],
        compiler_params=params,
        cost_estimate=pl.CostEstimate(
            flops=18 * count * rows * width, bytes_accessed=1 << 23, transcendentals=0
        ),
        name="attention",
    )(lengths, order, head, q, g, own, mine, other)
    dk, d_query = pl.pallas_call(
        functools.partial(own_slopes_kernel, width=width, group=group),
        out_shape=[
            jax.ShapeDtypeStruct((count, width), F32),
            jax.ShapeDtypeStruct((length, group * width), BF16),
        ],
        in_specs=[VM] * 6,
        out_specs=[VM] * 2,
        compiler_params=params,
        cost_estimate=pl.CostEstimate(
            flops=60 * count * rows * width, bytes_accessed=1 << 23, transcendentals=0
        ),
        name="own_slopes",
    )(q, g, mine, p_mine, rest, dq)
    return send, jnp.concatenate([dk, dv], axis=1), d_own, d_query


def per_device(query, resp_kv, grad_out, prefix_kv, lengths, order, *, layers, heads):
    width = resp_kv.shape[2] // 2
    shard = prefix_kv.shape[0]
    own = resp_kv[0]
    length = own.shape[0]

    def stack_heads(a):
        return jnp.transpose(a[0].reshape(length, -1, width), (1, 0, 2)).reshape(-1, width)

    q, g = stack_heads(query), stack_heads(grad_out)
    far = layers // 2
    to_core = [(i, i ^ 1) for i in range(4 * layers)]
    rings = [[4 * (2 * b + a) + i for b in range(far)] for a in range(2) for i in range(4)]
    squares = [[8 * b + 4 * a + 2 * x + c for a in range(2) for x in range(2)] for b in range(far) for c in range(2)]

    def exchange(array, groups):
        return lax.all_to_all(
            array, "roll", split_axis=0, concat_axis=0, tiled=True, axis_index_groups=groups
        )

    def to_all(array, groups):
        copies = len(groups[0])
        sent = jnp.broadcast_to(array[None], (copies,) + array.shape)
        return exchange(sent, groups).reshape(copies * array.shape[0], array.shape[1])

    def terms_of_all(terms, groups):
        return exchange(terms.astype(BF16).reshape(len(groups[0]), -1, terms.shape[1]), groups)

    def total(terms):
        return jnp.sum(terms.astype(F32), axis=0)

    mine = to_all(to_all(prefix_kv, rings), squares)
    other = lax.ppermute(mine, "roll", to_core)

    head = lax.axis_index("head").astype(jnp.int32)
    send, keep, d_own, d_query = run_attention(
        lengths, order, head.reshape(1), heads, q, g, own, mine, other, width
    )
    got = lax.ppermute(send, "roll", to_core)
    terms = (keep + got).astype(BF16)
    terms, d_own = lax.optimization_barrier((terms, d_own))

    def swap_heads(blocks, bit):
        sent = [i for i in range(heads) if i & bit]
        swapped = lax.ppermute(
            jnp.stack([blocks[i] for i in sent]), "head", [(i, i ^ bit) for i in range(heads)]
        )
        return [swapped[sent.index(i)] if i & bit else blocks[i] for i in range(heads)]

    blocks = [d_own[i] for i in range(heads)]
    bits = [1 << i for i in range(heads.bit_length() - 1)]
    for bit in bits[:-1]:
        blocks = swap_heads(blocks, bit)
    terms = total(terms_of_all(terms, squares)).astype(BF16)
    terms, blocks = lax.optimization_barrier((terms, blocks))
    blocks = swap_heads(blocks, bits[-1])
    terms = terms_of_all(terms, rings)
    terms, blocks = lax.optimization_barrier((terms, blocks))
    d_prefix = total(terms)

    for bit in bits:
        odd = (head & bit) != 0
        blocks = [jnp.where(odd, blocks[i ^ bit], blocks[i]) for i in range(heads)]
    d_resp = jnp.concatenate(blocks, axis=1)
    return d_query[None], d_resp[None], d_prefix


def solution(mesh):
    layers = mesh.shape["roll"] // 4
    return jax.shard_map(
        functools.partial(per_device, layers=layers, heads=mesh.shape["head"]),
        mesh=mesh,
        in_specs=(
            P("roll", None, "head"),
            P("roll", None, "head"),
            P("roll", None, "head"),
            P("roll", "head"),
            P(),
            P("roll"),
        ),
        out_specs=(P("roll", None, "head"), P("roll", "head", None), P("roll", "head")),
        check_vma=False,
    )
```
